128 devices in a mesh: scen: 16 (over y, x), base: 8 (over z, core).
Axes of the slice: x: 4, y: 4, z: 4, core: 2. Of those that a mesh axis runs over, the one named last changes fastest.
Arguments:
- right_sides: float32 [32, 8192], P(None, 'scen'), may hold values from -6 to 6
- base_hessian: float32 [8192], P('scen'), may hold values from 0.05 to 1
- sensitivity: float32 [32, 8192, 128], P('base', 'scen'), may hold values from -0.125 to 0.125
- weights: float32 [32, 128], P('base'), may hold values from 0.1 to 10
- outage_factors: float32 [32, 128], P('base'), may hold values from -1 to 1
- outaged: int32 [32], P('base'), may hold values from 0 to 127
Outputs:
- step: float32 [32, 8192], P(None, 'scen')
- flow_step: float32 [32, 32, 128], P('base')
The draws below stay inside these ranges and needn't reach their ends.
All inputs are finite; a program needn't handle non-finite values.
Results may differ from the reference program's by a relative error of at most 0.0003.
Values sent between devices are 32-bit elements; how exact they have to be, the bound alone decides.
A program may use at most 64 MiB of HBM per device.

```python
import math
import jax
import jax.numpy as jnp
from jax import lax

NVAR = 8192
LINES = 128
RHS = 32
ITERS = 5
CONT = 32


def touch_ends(values, stream_key, smallest, largest):
    longest = values.shape.index(max(values.shape))
    spots = []
    for shift in (0, 1):
        where = [jax.random.randint(jax.random.fold_in(stream_key, axis), (), 0, length) for axis, length in enumerate(values.shape)]
        where[longest] = (where[longest] + shift) % values.shape[longest]
        spots.append(tuple(where))
    return values.at[spots[0]].set(smallest).at[spots[1]].set(largest)


def with_spikes(drawn, rng, source, target, parts, factor):
    owner, partner = [(jnp.arange(drawn.shape[axis_at]) // (drawn.shape[axis_at] // parts)).reshape([-1 if axis == axis_at else 1 for axis in range(drawn.ndim)]) for axis_at in (source, target)]
    chosen = jax.random.permutation(rng, parts)[partner]
    strong = (owner == chosen) | (owner == (partner + parts // 2) % parts)
    return jnp.where(strong, factor * drawn, drawn)


def levels(own_key, shape, shards, smallest, largest):
    gain, own = 1.0, jax.random.fold_in(own_key, 6)
    for dim, parts in shards:
        heights = jnp.exp(jax.random.uniform(jax.random.fold_in(own, dim), (parts,), jnp.float32, smallest / len(shards), largest / len(shards)))
        gain = gain * jnp.repeat(heights, shape[dim] // parts).reshape([-1 if axis == dim else 1 for axis in range(len(shape))])
    return gain


def noise(key, extent, deviation, reach, cuts=(), held_as=jnp.bfloat16):
    gain = levels(key, extent, cuts, -0.22, 0.18) if cuts else 1.0
    result = jax.random.normal(key, extent, jnp.float32) * deviation * gain
    return jnp.minimum(jnp.maximum(result, -reach), reach).astype(held_as)


def heavy_noise(own_key, dims, scale, bound, shards, heavy, kind=jnp.bfloat16):
    result = scale * jax.random.normal(own_key, dims, jnp.float32)
    if shards:
        result = result * levels(own_key, dims, shards, -0.22, 0.18)
    return jnp.clip(with_spikes(result, jax.random.fold_in(own_key, 3), *heavy), -bound, bound).astype(kind)


def setup_inputs(seed: int = 0) -> dict:
    seeds = jax.random.split(jax.random.key(seed), 7)
    return {
        "right_sides": noise(seeds[0], (RHS, NVAR), 1.0, 6.0, ((1, 16),), jnp.float32),
        "base_hessian": jnp.clip(jnp.exp(math.log(1.0) - 2.9957323 * jax.random.uniform(seeds[1], (NVAR,), jnp.float32) ** levels(seeds[1], (NVAR,), ((0, 16),), -0.2, 0.2)), 0.05, 1.0),
        "sensitivity": heavy_noise(seeds[2], (CONT, NVAR, LINES), (CONT * LINES) ** -0.5, 0.125, ((0, 8), (1, 16)), (0, 1, 16, 2.0), jnp.float32),
        "weights": jnp.clip(jnp.exp(math.log(10.0) - 4.6051702 * jax.random.uniform(seeds[3], (CONT, LINES), jnp.float32) ** levels(seeds[3], (CONT, LINES), ((0, 8),), -0.2, 0.2)), 0.1, 10.0),
        "outage_factors": jnp.clip(jax.random.uniform(seeds[4], (CONT, LINES), jnp.float32, -1.0, 1.0) * levels(seeds[4], (CONT, LINES), ((0, 8),), -0.4, 0.0), -1.0, 1.0),
        "outaged": touch_ends(jax.random.randint(seeds[5], (CONT,), 0, LINES), jax.random.fold_in(seeds[5], 1), 0, LINES - 1).astype(jnp.int32),
    }


HIGHEST_PREC = lax.Precision.HIGHEST


def contingency_terms(flows_sum, weights, selector, factors):
    outaged_flow = jnp.sum(flows_sum * selector[:, None, :], axis=2, keepdims=True)
    post_flows = flows_sum + factors[:, None, :] * outaged_flow
    weighted = weights[:, None, :] * post_flows
    outaged_sum = jnp.sum(factors[:, None, :] * weighted, axis=2, keepdims=True)
    spread_back = weighted + selector[:, None, :] * outaged_sum
    return post_flows, weighted, spread_back


def reference(right_sides, base_hessian, sensitivity, weights, outage_factors, outaged):
    chosen = lax.broadcasted_iota(jnp.int32, weights.shape, 1) == outaged[:, None].astype(jnp.int32)
    selector = chosen.astype(weights.dtype)
    factors = jnp.where(chosen, -1.0, outage_factors).astype(weights.dtype)

    def apply_schur(direction):
        flows_sum = jnp.einsum('knm,rn->krm', sensitivity, direction, precision=HIGHEST_PREC)
        post_flows, weighted, spread_back = contingency_terms(flows_sum, weights, selector, factors)
        product = jnp.einsum('knm,krm->rn', sensitivity, spread_back, precision=HIGHEST_PREC)
        return product + base_hessian[None, :] * direction, weighted

    solution = jnp.zeros_like(right_sides)
    residual = right_sides
    direction = right_sides
    norm_now = jnp.sum(residual * residual, axis=1)
    for iteration in range(ITERS):
        product, unused = apply_schur(direction)
        step_len = norm_now / jnp.sum(direction * product, axis=1)
        solution = solution + step_len[:, None] * direction
        residual = residual - step_len[:, None] * product
        norm_next = jnp.sum(residual * residual, axis=1)
        direction = residual + (norm_next / norm_now)[:, None] * direction
        norm_now = norm_next
    flows_sum = jnp.einsum('knm,rn->krm', sensitivity, solution, precision=HIGHEST_PREC)
    post_flows, weighted, spread_back = contingency_terms(flows_sum, weights, selector, factors)
    return solution, weighted
```

```python
import functools

import jax
import jax.numpy as jnp
from jax import lax
from jax.experimental import pallas as pl
from jax.experimental.pallas import tpu as pltpu
from jax.sharding import PartitionSpec as P

ITERS = 5
MESH = pl.DeviceIdType.MESH
F32 = jnp.float32
BF16 = jnp.bfloat16


def halves(value):
    high = value.astype(BF16)
    return high, (value - high.astype(F32)).astype(BF16)


def kernel(S, B, b_ref, h_ref, a_ref, w_ref, f_ref, o_ref, x_ref, y_ref,
           c_hi, c_lo, lhs, flow_out, flow_in, total, image_out, image_in, resid,
           p_ref, w_own, gp_ref, gs_ref, send, recv):
    K, N, M = a_ref.shape
    R = b_ref.shape[0]
    Q = R // 8
    H = B // Q
    W = N // H
    s = lax.axis_index("scen")
    b = lax.axis_index("base")

    barrier = pltpu.get_barrier_semaphore()
    for d in range(1, S):
        pl.semaphore_signal(barrier, inc=1, device_id=(lax.rem(s + d, S), b), device_id_type=MESH)
    for d in range(1, B):
        pl.semaphore_signal(barrier, inc=1, device_id=(s, lax.rem(b + d, B)), device_id_type=MESH)

    lane_m = lax.broadcasted_iota(jnp.int32, (1, M), 1)
    for k in range(K):
        chosen = lane_m == o_ref[k]
        root = jnp.sqrt(w_ref[k : k + 1, :])
        factor = jnp.where(chosen, -1.0, f_ref[k : k + 1, :]) * root
        a = a_ref[k]
        at = jnp.sum(jnp.where(chosen, a, 0.0), axis=1, keepdims=True)
        hi, lo = halves(a * root + at * factor)
        c_hi[:, k * M : (k + 1) * M] = hi
        c_lo[:, k * M : (k + 1) * M] = lo

    for q in range(Q):
        for t in range(H):
            resid[0, H * q + t] = b_ref[8 * q : 8 * q + 8, t * W : (t + 1) * W]
    x_ref[...] = jnp.zeros_like(x_ref)
    p_ref[...] = jnp.zeros_like(p_ref)
    w_own[...] = jnp.zeros_like(w_own)
    gp_ref[...] = jnp.zeros_like(gp_ref)
    gs_ref[...] = jnp.zeros_like(gs_ref)

    lane = lax.broadcasted_iota(jnp.int32, (8, 128), 1)
    sub = lax.broadcasted_iota(jnp.int32, (8, 128), 0)

    def row_of(columns, base):
        out = jnp.zeros((8, 128), F32)
        for q in range(Q):
            out = out + jnp.where(lane == sub + (base + 8 * q), columns[q], 0.0)
        return jnp.sum(out, axis=0, keepdims=True)

    def column_of(row, base):
        return jnp.sum(jnp.where(lane == sub + base, row, 0.0), axis=1, keepdims=True)

    def sends(phase, count, axis, src, dst):
        for d in range(1, count):
            if axis == "scen":
                to = lax.rem(s + d, count)
                device = (to, b)
            else:
                to = lax.rem(b + d, count)
                device = (s, to)
            pltpu.make_async_remote_copy(
                src_ref=src(to), dst_ref=dst(to), send_sem=send.at[phase], recv_sem=recv.at[phase],
                device_id=device, device_id_type=MESH,
            ).start()

    def waits(sems, phase, ref):
        pltpu.make_async_copy(ref, ref, sems.at[phase]).wait()

    def flows(now):
        rows = []
        squares, bent = [], []
        for q in range(Q):
            r = jnp.concatenate([resid[now, H * q + t] for t in range(H)], axis=1)
            rows.append(r)
            rr = r * r
            squares.append(jnp.sum(rr, axis=1, keepdims=True))
            bent.append(jnp.sum(rr * h_ref[...], axis=1, keepdims=True))
        hi, lo = halves(jnp.concatenate(rows, axis=0))
        lhs[:R, :] = hi
        lhs[R:, :] = lo
        big = jnp.dot(lhs[...], c_hi[...], preferred_element_type=F32)
        part = big[:R] + big[R:] + jnp.dot(lhs[:R], c_lo[...], preferred_element_type=F32)
        for k in range(K):
            for q in range(Q):
                flow_out[k * Q + q] = part[8 * q : 8 * q + 8, k * M : (k + 1) * M]
        sends(0, S, "scen", lambda to: flow_out.at[to], lambda to: flow_in.at[s])
        flow_in[s] = flow_out[s]
        scalars = row_of(squares, 0) + row_of(bent, R)
        total[s, 8:9, :] = scalars
        waits(recv, 0, flow_in.at[pl.ds(0, S - 1)])
        tile = flow_in[0]
        for t in range(1, S):
            tile = tile + flow_in[t]
        total[s, 0:8, :] = tile
        sends(1, S, "scen", lambda to: total.at[s, pl.ds(0, 9)], lambda to: total.at[s, pl.ds(0, 9)])
        waits(send, 0, flow_out.at[pl.ds(0, S - 1)])
        waits(recv, 1, total.at[pl.ds(0, S - 1), pl.ds(0, 9)])
        waits(send, 1, total.at[pl.ds(0, S - 1), pl.ds(0, 9)])
        row = total[0, 8:9, :]
        for t in range(1, S):
            row = row + total[t, 8:9, :]
        g = [[total[k * Q + q, 0:8, :] for k in range(K)] for q in range(Q)]
        curv = []
        for q in range(Q):
            squared = g[q][0] * g[q][0]
            for k in range(1, K):
                squared = squared + g[q][k] * g[q][k]
            curv.append(jnp.sum(squared, axis=1, keepdims=True))
        return g, row, row_of(curv, 2 * R)

    def coefficients(first, row, rest, gamma_old, alpha_old):
        out = []
        for q in range(Q):
            gamma = column_of(row, 8 * q)
            beta = jnp.where(first, 0.0, gamma / gamma_old[q])
            delta = column_of(rest, 8 * q)
            alpha = gamma / (delta - beta * (gamma / alpha_old[q]))
            out.append((gamma, beta, alpha))
        return out

    def move(now, g, coef):
        for q in range(Q):
            _, beta, alpha = coef[q]
            for t in range(H):
                p = resid[now, H * q + t] + beta * p_ref[H * q + t]
                p_ref[H * q + t] = p
                rows, cols = slice(8 * q, 8 * q + 8), slice(t * W, (t + 1) * W)
                x_ref[rows, cols] = x_ref[rows, cols] + alpha * p
            for k in range(K):
                gp = g[q][k] + beta * gp_ref[k, 8 * q : 8 * q + 8, :]
                gp_ref[k, 8 * q : 8 * q + 8, :] = gp
                gs_ref[k, 8 * q : 8 * q + 8, :] = gs_ref[k, 8 * q : 8 * q + 8, :] + alpha * gp

    pl.semaphore_wait(barrier, S - 1 + B - 1)

    mine_q = b // H
    mine_t = lax.rem(b, H)
    nt = (((1,), (1,)), ((), ()))

    def step(i, carry):
        gamma_old, alpha_old = carry
        now, later = lax.rem(i, 2), lax.rem(i + 1, 2)
        g, row, curv = flows(now)
        hi, lo = halves(jnp.concatenate([jnp.concatenate(g[q], axis=1) for q in range(Q)], axis=0))
        lhs[:R, :] = hi
        lhs[R:, :] = lo
        big = lax.dot_general(lhs[...], c_hi[...], nt, preferred_element_type=F32)
        part = big[:R] + big[R:] + lax.dot_general(lhs[:R], c_lo[...], nt, preferred_element_type=F32)
        for q in range(Q):
            for t in range(H):
                for v in range(W // 128):
                    image_out[H * q + t, 8 * v : 8 * v + 8, :] = part[
                        8 * q : 8 * q + 8, t * W + v * 128 : t * W + (v + 1) * 128
                    ]
        L = W // 128 * 8
        for j in range(B):
            image_out[j, L : L + 1, :] = curv
        sends(2, B, "base", lambda to: image_out.at[to, pl.ds(0, L + 1)], lambda to: image_in.at[b, pl.ds(0, L + 1)])
        image_in[b] = image_out[b]
        waits(recv, 2, image_in.at[pl.ds(0, B - 1), pl.ds(0, L + 1)])
        summed = image_in[0]
        for t in range(1, B):
            summed = summed + image_in[t]
        rest = pltpu.roll(row, 128 - R, 1) + pltpu.roll(summed[L : L + 1, :], 128 - 2 * R, 1)
        coef = coefficients(i == 0, row, rest, gamma_old, alpha_old)
        beta, alpha = coef[0][1], coef[0][2]
        for q in range(1, Q):
            beta = jnp.where(mine_q == q, coef[q][1], beta)
            alpha = jnp.where(mine_q == q, coef[q][2], alpha)
        r = resid[now, b]
        hess = h_ref[:, pl.ds(pl.multiple_of(mine_t * W, W), W)]
        image = jnp.concatenate([summed[8 * v : 8 * v + 8] for v in range(W // 128)], axis=1)
        w = image + hess * r + beta * w_own[...]
        w_own[...] = w
        resid[later, b] = r - alpha * w
        sends(3, B, "base", lambda to: resid.at[later, b], lambda to: resid.at[later, b])
        move(now, g, coef)
        waits(send, 2, image_out.at[pl.ds(0, B - 1), pl.ds(0, L + 1)])
        waits(recv, 3, resid.at[0, pl.ds(0, B - 1)])
        waits(send, 3, resid.at[0, pl.ds(0, B - 1)])
        return [c[0] for c in coef], [c[2] for c in coef]

    ones = [jnp.ones((8, 1), F32)] * Q
    gamma_old, alpha_old = lax.fori_loop(0, ITERS - 1, step, (ones, ones))

    now = (ITERS - 1) % 2
    g, row, curv = flows(now)
    image_out[0, 0:1, :] = curv
    image_in[b, 0:1, :] = curv
    sends(2, B, "base", lambda to: image_out.at[0, pl.ds(0, 1)], lambda to: image_in.at[b, pl.ds(0, 1)])
    waits(recv, 2, image_in.at[pl.ds(0, B - 1), pl.ds(0, 1)])
    rest = image_in[0, 0:1, :]
    for t in range(1, B):
        rest = rest + image_in[t, 0:1, :]
    rest = pltpu.roll(row, 128 - R, 1) + pltpu.roll(rest, 128 - 2 * R, 1)
    coef = coefficients(False, row, rest, gamma_old, alpha_old)
    move(now, g, coef)
    for k in range(K):
        y_ref[k] = gs_ref[k] * jnp.sqrt(w_ref[k : k + 1, :])
    waits(send, 2, image_out.at[pl.ds(0, B - 1), pl.ds(0, 1)])


def per_device(S, B, right_sides, base_hessian, sensitivity, weights, outage_factors, outaged):
    K, N, M = sensitivity.shape
    R = right_sides.shape[0]
    Q = R // 8
    H = B // Q
    W = N // H
    vmem = pl.BlockSpec(memory_space=pltpu.VMEM)
    tall = W // 128 * 8 + 8
    return pl.pallas_call(
        functools.partial(kernel, S, B),
        out_shape=(jax.ShapeDtypeStruct((R, N), F32), jax.ShapeDtypeStruct((K, R, M), F32)),
        in_specs=[vmem] * 5 + [pl.BlockSpec(memory_space=pltpu.SMEM)],
        out_specs=(vmem, vmem),
        scratch_shapes=[
            pltpu.VMEM((N, K * M), BF16),
            pltpu.VMEM((N, K * M), BF16),
            pltpu.VMEM((2 * R, max(N, K * M)), BF16),
            pltpu.VMEM((S, 8, 128), F32),
            pltpu.VMEM((S, 8, 128), F32),
            pltpu.VMEM((S, 16, 128), F32),
            pltpu.VMEM((B, tall, 128), F32),
            pltpu.VMEM((B, tall, 128), F32),
            pltpu.VMEM((2, B, 8, W), F32),
            pltpu.VMEM((B, 8, W), F32),
            pltpu.VMEM((8, W), F32),
            pltpu.VMEM((K, R, M), F32),
            pltpu.VMEM((K, R, M), F32),
            pltpu.SemaphoreType.DMA((4,)),
            pltpu.SemaphoreType.DMA((4,)),
        ],
        compiler_params=pltpu.CompilerParams(
            collective_id=0, has_side_effects=True, vmem_limit_bytes=32 * 1024 * 1024
        ),
    )(right_sides, base_hessian.reshape(1, N), sensitivity, weights, outage_factors, outaged)


def solution(mesh):
    placed = (
        P(None, "scen"),
        P("scen"),
        P("base", "scen", None),
        P("base", None),
        P("base", None),
        P("base"),
    )
    return jax.shard_map(
        functools.partial(per_device, mesh.shape["scen"], mesh.shape["base"]),
        mesh=mesh,
        in_specs=placed,
        out_specs=(P(None, "scen"), P("base", None, None)),
        check_vma=False,
    )
```
